32 devices in a mesh: seq: 8 (over z, x), head: 4 (over y, core).
Axes of the slice: x: 2, y: 2, z: 4, core: 2. Of those that a mesh axis runs over, the one named last changes fastest.
Arguments:
- query_rows: float32 [4096, 1024], P('seq', 'head'), may hold values from -128 to 128
- key_rows: float32 [4096, 1024], P('seq', 'head'), may hold values from -128 to 128
- value_rows: float32 [4096, 1024], P('seq', 'head'), may hold values from -6 to 6
- teacher_out: float32 [4096, 1024], P(('seq', 'head')), may hold values from -6 to 6
- query_map: float32 [4, 256, 256], P('head'), may hold values from -1 to 1
- key_map: float32 [4, 256, 256], P('head'), may hold values from -1 to 1
- block_map: int32 [8, 8], replicated, may hold values from 0 to 63, as said below
Outputs:
- grad_query_map: float32 [4, 256, 256], P('head', 'seq')
- grad_key_map: float32 [4, 256, 256], P('head', 'seq')
The draws below stay inside these ranges and needn't reach their ends.
Inputs may be any that keep to these rules, and one draw needn't show every extreme that they name: `block_map`: row d lists, slot by slot, the sequence blocks whose teacher rows storage row group d holds (storage block d * 8 + j). Sequence block b belongs to owner b // 8. Every row names exactly one block of each owner, and every block appears exactly once in the table.
All inputs are finite; a program needn't handle non-finite values.
Results may differ from the reference program's by a relative error of at most 0.00035.
Values sent between devices are 32-bit elements; how exact they have to be, the bound alone decides.
A program may use at most 128 MiB of HBM per device.

```python
import jax
import jax.numpy as jnp
from jax import lax

E = 256
HEADS = 4
FH = 256
TOK_DEV = 512
SEQ = 4096
OWNERS = 8
BLK = 64


def weights_for(key, which):
    return jax.random.normal(jax.random.fold_in(key, 11 + which), (HEADS, E, FH), jnp.float32) * E ** (-0.5)


def draw_rows(key, which):
    base_rows = jnp.clip(jax.random.normal(jax.random.fold_in(key, 21 + which), (SEQ, HEADS * E), jnp.float32), -6.0, 6.0)
    return base_rows


def draw_query_rows(key, part):
    return draw_rows(key, 0)


def draw_key_rows(key, part):
    return draw_rows(key, 1)


def draw_query_map(key, part):
    return weights_for(key, 0)


def draw_key_map(key, part):
    return weights_for(key, 1)


def draw_block_map(key, part):
    owner_keys = jax.random.split(jax.random.fold_in(key, 41), OWNERS)
    slot_keys = jax.random.split(jax.random.fold_in(key, 42), OWNERS)
    within_order = jax.vmap(lambda sub_key: jax.random.permutation(sub_key, OWNERS))(owner_keys)
    slot_owner = jax.vmap(lambda sub_key: jax.random.permutation(sub_key, OWNERS))(slot_keys)
    within_by_device = jnp.transpose(within_order)
    picked = jnp.take_along_axis(within_by_device, slot_owner, axis=1)
    return (slot_owner * OWNERS + picked).astype(jnp.int32)


def levels(key, extent, shards, least, largest):
    loudness = 1.0
    for position, blocks in shards:
        draws = jax.random.uniform(jax.random.fold_in(jax.random.fold_in(key, 6), position), (blocks,), jnp.float32, least / len(shards), largest / len(shards))
        loudness = loudness * jnp.repeat(jnp.exp(draws), extent[position] // blocks).reshape((-1,) + (1,) * (len(extent) - 1 - position))
    return loudness


def scatter_about(own_key, dims, scale, limit, cuts=(), kind=jnp.bfloat16):
    level = levels(own_key, dims, cuts, -0.22, 0.18) if cuts else 1.0
    values = jax.random.normal(own_key, dims, jnp.float32) * scale * level
    return jnp.minimum(jnp.maximum(values, -limit), limit).astype(kind)


def setup_inputs(seed: int = 0) -> dict:
    arg_keys = jax.random.split(jax.random.key(seed), 8)
    return {
        "query_rows": draw_query_rows(jax.random.fold_in(arg_keys[7], 71), 0),
        "key_rows": draw_key_rows(jax.random.fold_in(arg_keys[7], 71), 0),
        "value_rows": scatter_about(arg_keys[2], (SEQ, HEADS * E), 1.0, 6.0, ((0, 8), (1, 4)), jnp.float32),
        "teacher_out": scatter_about(arg_keys[3], (SEQ, HEADS * E), 1.0, 6.0, ((0, 32),), jnp.float32),
        "query_map": draw_query_map(jax.random.fold_in(arg_keys[7], 71), 0),
        "key_map": draw_key_map(jax.random.fold_in(arg_keys[7], 71), 0),
        "block_map": draw_block_map(jax.random.fold_in(arg_keys[7], 71), 0),
    }


exact_prec = lax.Precision.HIGHEST


def back_pair(first_half, second_half, grad_feat, half_feat):
    grad_first = grad_feat[..., :half_feat]
    grad_second = grad_feat[..., half_feat:]
    lead = first_half * (grad_first - jnp.sum(first_half * grad_first, axis=-1, keepdims=True))
    trail = second_half * (grad_second - jnp.sum(second_half * grad_second, axis=-1, keepdims=True))
    return lead - trail


def head_grads(queries, keys_in, values_in, target, map_q, map_k):
    pre_q = jnp.dot(queries, map_q, precision=exact_prec, preferred_element_type=jnp.float32)
    pre_k = jnp.dot(keys_in, map_k, precision=exact_prec, preferred_element_type=jnp.float32)
    first_q = jax.nn.softmax(pre_q, axis=-1)
    second_q = jax.nn.softmax(-pre_q, axis=-1)
    first_k = jax.nn.softmax(pre_k, axis=-1)
    second_k = jax.nn.softmax(-pre_k, axis=-1)
    feat_q = jnp.concatenate([first_q, second_q], axis=-1)
    feat_k = jnp.concatenate([first_k, second_k], axis=-1)
    blocks = SEQ // TOK_DEV
    features = 2 * FH
    q_blocks = feat_q.reshape(blocks, TOK_DEV, features)
    k_blocks = feat_k.reshape(blocks, TOK_DEV, features)
    v_blocks = values_in.reshape(blocks, TOK_DEV, E)
    t_blocks = target.reshape(blocks, TOK_DEV, E)
    ladder = jnp.arange(TOK_DEV, dtype=jnp.int32)
    causal = (ladder[:, None] >= ladder[None, :]).astype(jnp.float32)
    zero_pair = (jnp.zeros((features, E), jnp.float32), jnp.zeros((features,), jnp.float32))

    def forward(state_pair, inputs):
        prev_state, prev_norm = state_pair
        blk_q, blk_k, values_b, target_b = inputs
        scores = jnp.dot(blk_q, blk_k.T, precision=exact_prec, preferred_element_type=jnp.float32) * causal
        numerator = jnp.dot(scores, values_b, precision=exact_prec, preferred_element_type=jnp.float32)
        numerator = numerator + jnp.dot(blk_q, prev_state, precision=exact_prec, preferred_element_type=jnp.float32)
        raw_sum = jnp.sum(scores, axis=1) + jnp.dot(blk_q, prev_norm, precision=exact_prec, preferred_element_type=jnp.float32)
        divisor = jnp.maximum(raw_sum, 1.0)
        student = numerator / divisor[:, None]
        mismatch = student - target_b
        grad_num = mismatch / divisor[:, None]
        grad_div = jnp.where(raw_sum > 1.0, -jnp.sum(mismatch * student, axis=1) / divisor, 0.0)
        new_state = prev_state + jnp.dot(blk_k.T, values_b, precision=exact_prec, preferred_element_type=jnp.float32)
        new_norm = prev_norm + jnp.sum(blk_k, axis=0)
        return (new_state, new_norm), (prev_state, prev_norm, grad_num, grad_div)

    unused_pair, saved = lax.scan(forward, zero_pair, (q_blocks, k_blocks, v_blocks, t_blocks))
    prev_states, prev_norms, grad_nums, grad_divs = saved

    def backward(state_pair, inputs):
        next_state, next_norm = state_pair
        blk_q, blk_k, values_b, prev_state, prev_norm, grad_num, grad_div = inputs
        weights = (jnp.dot(grad_num, values_b.T, precision=exact_prec, preferred_element_type=jnp.float32) + grad_div[:, None]) * causal
        grad_fq = jnp.dot(weights, blk_k, precision=exact_prec, preferred_element_type=jnp.float32)
        grad_fq = grad_fq + jnp.dot(grad_num, prev_state.T, precision=exact_prec, preferred_element_type=jnp.float32)
        grad_fq = grad_fq + grad_div[:, None] * prev_norm[None, :]
        grad_fk = jnp.dot(weights.T, blk_q, precision=exact_prec, preferred_element_type=jnp.float32)
        grad_fk = grad_fk + jnp.dot(values_b, next_state.T, precision=exact_prec, preferred_element_type=jnp.float32)
        grad_fk = grad_fk + next_norm[None, :]
        new_state = next_state + jnp.dot(blk_q.T, grad_num, precision=exact_prec, preferred_element_type=jnp.float32)
        new_norm = next_norm + jnp.dot(grad_div, blk_q, precision=exact_prec, preferred_element_type=jnp.float32)
        return (new_state, new_norm), (grad_fq, grad_fk)

    unused_back, grads_blocks = lax.scan(backward, zero_pair, (q_blocks, k_blocks, v_blocks, prev_states, prev_norms, grad_nums, grad_divs), reverse=True)
    grad_fq = grads_blocks[0].reshape(SEQ, features)
    grad_fk = grads_blocks[1].reshape(SEQ, features)
    grad_pq = back_pair(first_q, second_q, grad_fq, FH)
    grad_pk = back_pair(first_k, second_k, grad_fk, FH)
    result_q = jnp.dot(queries.T, grad_pq, precision=exact_prec, preferred_element_type=jnp.float32)
    result_k = jnp.dot(keys_in.T, grad_pk, precision=exact_prec, preferred_element_type=jnp.float32)
    return result_q, result_k


def reference(query_rows, key_rows, value_rows, teacher_out, query_map, key_map, block_map):
    storage_order = jnp.argsort(block_map.reshape(-1)).astype(jnp.int32)
    stored_blocks = teacher_out.reshape(OWNERS * OWNERS, BLK, HEADS * E)
    teacher_seq = jnp.take(stored_blocks, storage_order, axis=0).reshape(SEQ, HEADS * E)
    query_heads = query_rows.reshape(SEQ, HEADS, E).transpose(1, 0, 2)
    key_heads = key_rows.reshape(SEQ, HEADS, E).transpose(1, 0, 2)
    value_heads = value_rows.reshape(SEQ, HEADS, E).transpose(1, 0, 2)
    target_heads = teacher_seq.reshape(SEQ, HEADS, E).transpose(1, 0, 2)

    def one_head(bundle):
        return head_grads(bundle[0], bundle[1], bundle[2], bundle[3], bundle[4], bundle[5])

    head_results = lax.map(one_head, (query_heads, key_heads, value_heads, target_heads, query_map, key_map))
    return head_results[0], head_results[1]
```

```python
import functools

import jax
import jax.numpy as jnp
from jax import lax
from jax.experimental import pallas as pl
from jax.experimental.pallas import tpu as pltpu
from jax.sharding import PartitionSpec as P

MESH = pl.DeviceIdType.MESH
F32 = jnp.float32
BF16 = jnp.bfloat16
NN = (((1,), (0,)), ((), ()))
NT = (((1,), (1,)), ((), ()))
TN = (((0,), (0,)), ((), ()))


def split(x):
    hi = x.astype(BF16)
    return hi, (x - hi.astype(F32)).astype(BF16)


def dot3(a, b, dims):
    one = functools.partial(
        lax.dot_general, dimension_numbers=dims, preferred_element_type=F32
    )
    return one(a[0], b[0]) + (one(a[0], b[1]) + one(a[1], b[0]))


def chunk_bounds(rows, count):
    units = rows // 8
    edges = [8 * (units * i // count) for i in range(count + 1)]
    return [(edges[i], edges[i + 1] - edges[i]) for i in range(count)]


def kernel(
    n, nh, chunks,
    q_ref, k_ref, v_ref, t_ref, qm_ref, km_ref, bm_ref,
    oq_ref, ok_ref,
    gath, t_send, t_arr, teach,
    vh, vl, fk, fkh, fkl, fq, fqh, fql,
    own, x1, part, chain, give, prev,
    grad_k, terms, rs,
    sem_t1, sem_t2, sem_x1, sem_p, sem_x2, sem_rs, sem_loc,
):
    tokens, width = q_ref.shape
    half = fk.shape[2]
    br = tokens // n
    group = t_ref.shape[0]
    er = width // n
    me = lax.axis_index("seq")
    mh = lax.axis_index("head")
    inner = 2
    outer = n // inner
    z = me // inner
    c = me % inner

    def seq_dev(i):
        return (i, mh)

    barrier = pltpu.get_barrier_semaphore()
    for d in range(1, n):
        pl.semaphore_signal(
            barrier, inc=1, device_id=seq_dev((me + d) % n), device_id_type=MESH
        )
    for d in range(1, nh):
        pl.semaphore_signal(
            barrier, inc=1, device_id=(me, (mh + d) % nh), device_id_type=MESH
        )
    pl.semaphore_wait(barrier, n - 1 + nh - 1)

    def t1_copy(to, frm):
        cols = pl.ds(pl.multiple_of(to * width, 128), width)
        return pltpu.make_async_remote_copy(
            src_ref=t_ref.at[:, cols],
            dst_ref=gath.at[pl.ds(pl.multiple_of(frm * group, 8), group), :],
            send_sem=sem_t1.at[0, to],
            recv_sem=sem_t1.at[1, frm],
            device_id=(me, to),
            device_id_type=MESH,
        )

    for d in range(1, nh):
        t1_copy((mh + d) % nh, mh).start()
    t1_own = pltpu.make_async_copy(
        t_ref.at[:, pl.ds(pl.multiple_of(mh * width, 128), width)],
        gath.at[pl.ds(pl.multiple_of(mh * group, 8), group), :],
        sem_loc.at[0],
    )
    t1_own.start()

    def features(rows_ref, map_ref, f, fh, fl):
        pre = jnp.dot(
            rows_ref[...], map_ref[...], precision=lax.Precision.HIGHEST,
            preferred_element_type=F32,
        )
        up = jnp.exp(pre - jnp.max(pre, axis=-1, keepdims=True))
        p1 = up / jnp.sum(up, axis=-1, keepdims=True)
        down = jnp.exp(jnp.min(pre, axis=-1, keepdims=True) - pre)
        p2 = down / jnp.sum(down, axis=-1, keepdims=True)
        for i, p in enumerate((p1, p2)):
            hi, lo = split(p)
            f[i] = p
            fh[i] = hi
            fl[i] = lo

    partner = seq_dev(z * inner + 1 - c)

    def swap_copy(way, i):
        rows = pl.ds(*chunks[i])
        return pltpu.make_async_remote_copy(
            src_ref=own.at[way, 1 - c, rows], dst_ref=x1.at[way, rows],
            send_sem=sem_x1.at[way, 0, i], recv_sem=sem_x1.at[way, 1, i],
            device_id=partner, device_id_type=MESH,
        )

    def onward_copy(way, i):
        rows = pl.ds(*chunks[i])
        zn = lax.rem(z + (1 if way == 0 else outer - 1), outer)
        return pltpu.make_async_remote_copy(
            src_ref=chain.at[way, rows], dst_ref=part.at[way, rows],
            send_sem=sem_p.at[way, 0, i], recv_sem=sem_p.at[way, 1, i],
            device_id=seq_dev(zn * inner + c), device_id_type=MESH,
        )

    def across_copy(way, i, which):
        rows = pl.ds(*chunks[i])
        return pltpu.make_async_remote_copy(
            src_ref=give.at[way, rows], dst_ref=prev.at[way, which, rows],
            send_sem=sem_x2.at[way, 0, i], recv_sem=sem_x2.at[way, 1, i],
            device_id=partner, device_id_type=MESH,
        )

    def scan_begin(way):
        for i in range(len(chunks)):
            swap_copy(way, i).start()

    def scan_run(way):
        place = z if way == 0 else outer - 1 - z
        leads = (c if way == 0 else 1 - c) == 0

        @pl.when(place == 0)
        def _():
            part[way] = jnp.zeros(part.shape[1:], F32)

        for i in range(len(chunks)):
            at, size = chunks[i]
            rows = pl.ds(at, size)
            swap_copy(way, i).wait_recv()

            @pl.when(place > 0)
            def _():
                onward_copy(way, i).wait_recv()

            @pl.when(place < outer - 1)
            def _():
                chain[way, rows] = part[way, rows] + (own[way, c, rows] + x1[way, rows])
                onward_copy(way, i).start()

            before = part[way, rows]
            give[way, rows] = before + jnp.where(leads, own[way, c, rows], 0.0)
            across_copy(way, i, c).start()
            prev[way, c, rows] = before + jnp.where(leads, 0.0, x1[way, rows])

    def scan_end(way):
        place = z if way == 0 else outer - 1 - z
        for i in range(len(chunks)):
            across_copy(way, i, 1 - c).wait_recv()
            swap_copy(way, i).wait_send()
            across_copy(way, i, c).wait_send()

            @pl.when(place < outer - 1)
            def _():
                onward_copy(way, i).wait_send()

    def put_state(way, which, value, norm):
        own[way, which, 0:width] = value
        own[way, which, width:width + 8] = jnp.broadcast_to(norm, (8, half))

    features(k_ref, km_ref, fk, fkh, fkl)
    v_hi, v_lo = split(v_ref[...])
    vh[...] = v_hi
    vl[...] = v_lo

    def key_state(which):
        put_state(
            0, which,
            dot3((vh[...], vl[...]), (fkh[which], fkl[which]), TN),
            jnp.sum(fk[which], axis=0, keepdims=True),
        )

    key_state(1 - c)
    scan_begin(0)
    key_state(c)

    for d in range(1, nh):
        frm = (mh + d) % nh
        t1_copy(frm, frm).wait_recv()
    t1_own.wait()

    def t2_copy(to, frm):
        return pltpu.make_async_remote_copy(
            src_ref=t_send.at[to],
            dst_ref=t_arr.at[frm],
            send_sem=sem_t2.at[0, to],
            recv_sem=sem_t2.at[1, frm],
            device_id=seq_dev(to),
            device_id_type=MESH,
        )

    mine = bm_ref[pl.ds(me, 1), :]
    for d in range(n):
        to = (me + d) % n
        held = ((mine >= to * n) & (mine < to * n + n)).astype(F32)
        block = jnp.zeros((br, width), F32)
        for j in range(n):
            block = block + held[:, j:j + 1] * gath[j * br:(j + 1) * br]
        if d == 0:
            t_arr[me] = block
        else:
            t_send[to] = block
            t2_copy(to, me).start()

    features(q_ref, qm_ref, fq, fqh, fql)
    causal = (
        lax.broadcasted_iota(jnp.int32, (tokens, tokens), 0)
        >= lax.broadcasted_iota(jnp.int32, (tokens, tokens), 1)
    )
    scores = dot3((fqh[0], fql[0]), (fkh[0], fkl[0]), NT)
    scores = scores + dot3((fqh[1], fql[1]), (fkh[1], fkl[1]), NT)
    scores = jnp.where(causal, scores, 0.0)
    numerator = dot3(split(scores), (vh[...], vl[...]), NN)
    raw_sum = jnp.sum(scores, axis=-1, keepdims=True)

    scan_run(0)
    scan_end(0)

    for i in range(2):
        numerator = numerator + dot3(
            (fqh[i], fql[i]), split(prev[0, i, 0:width]), NT
        )
        raw_sum = raw_sum + jnp.sum(
            fq[i] * prev[0, i, width:width + 1], axis=-1, keepdims=True
        )
    divisor = jnp.maximum(raw_sum, 1.0)
    student = numerator / divisor

    for d in range(1, n):
        frm = (me + d) % n
        t2_copy(frm, frm).wait_recv()
    table = bm_ref[...]
    owned = (table >= me * n) & (table < me * n + n)
    within = jnp.sum(
        jnp.where(owned, table - me * n, 0).astype(F32), axis=1, keepdims=True
    )
    for w in range(n):
        found = (within == w).astype(F32)
        block = jnp.zeros((br, width), F32)
        for s in range(n):
            block = block + found[s:s + 1, :] * t_arr[s]
        teach[w * br:(w + 1) * br] = block

    mismatch = student - teach[...]
    grad_num = mismatch / divisor
    grad_div = jnp.where(
        raw_sum > 1.0,
        -jnp.sum(mismatch * student, axis=-1, keepdims=True) / divisor,
        0.0,
    )
    gn = split(grad_num)

    def query_state(which):
        put_state(
            1, which,
            dot3(gn, (fqh[which], fql[which]), TN),
            jnp.sum(grad_div * fq[which], axis=0, keepdims=True),
        )

    query_state(1 - c)
    scan_begin(1)
    query_state(c)

    weights = dot3(gn, (vh[...], vl[...]), NT) + grad_div
    w_parts = split(jnp.where(causal, weights, 0.0))
    grad_q = []
    for i in range(2):
        g = dot3(w_parts, (fkh[i], fkl[i]), NN)
        g = g + dot3(gn, split(prev[0, i, 0:width]), NN)
        grad_q.append(g + grad_div * prev[0, i, width:width + 1])
        grad_k[i] = dot3(w_parts, (fqh[i], fql[i]), TN)

    def back_pair(f, g1, g2):
        p1, p2 = f[0], f[1]
        lead = p1 * (g1 - jnp.sum(p1 * g1, axis=-1, keepdims=True))
        trail = p2 * (g2 - jnp.sum(p2 * g2, axis=-1, keepdims=True))
        return lead - trail

    def rs_copy(i, to, frm):
        return pltpu.make_async_remote_copy(
            src_ref=terms.at[i, pl.ds(pl.multiple_of(to * er, 8), er), :],
            dst_ref=rs.at[i, frm],
            send_sem=sem_rs.at[i, 0, to],
            recv_sem=sem_rs.at[i, 1, frm],
            device_id=seq_dev(to),
            device_id_type=MESH,
        )

    def rs_begin(i, rows_ref, grad):
        terms[i] = dot3(split(rows_ref[...]), split(grad), TN)
        for d in range(1, n):
            rs_copy(i, (me + d) % n, me).start()

    def rs_finish(i, out_ref):
        total = terms[i, pl.ds(pl.multiple_of(me * er, 8), er), :]
        for d in range(1, n):
            frm = (me + d) % n
            rs_copy(i, frm, frm).wait_recv()
            total = total + rs[i, frm]
        out_ref[0] = total

    grad_pq = back_pair(fq, grad_q[0], grad_q[1])

    scan_run(1)
    rs_begin(0, q_ref, grad_pq)
    scan_end(1)

    grads = []
    for i in range(2):
        g = grad_k[i] + dot3((vh[...], vl[...]), split(prev[1, i, 0:width]), NN)
        grads.append(g + prev[1, i, width:width + 1])
    rs_begin(1, k_ref, back_pair(fk, grads[0], grads[1]))
    rs_finish(0, oq_ref)
    rs_finish(1, ok_ref)

    for d in range(1, nh):
        t1_copy((mh + d) % nh, mh).wait_send()
    for d in range(1, n):
        to = (me + d) % n
        t2_copy(to, me).wait_send()
        rs_copy(0, to, me).wait_send()
        rs_copy(1, to, me).wait_send()


def per_device(n, nh, query_rows, key_rows, value_rows, teacher_out, query_map, key_map, block_map):
    tokens, width = query_rows.shape
    half = query_map.shape[2]
    group = teacher_out.shape[0]
    er = width // n
    br = tokens // n
    rows = width + 8
    chunks = chunk_bounds(rows, 6)
    count = len(chunks)
    vmem = pl.BlockSpec(memory_space=pltpu.VMEM)
    dma = pltpu.SemaphoreType.DMA
    feat = [
        pltpu.VMEM((2, tokens, half), F32),
        pltpu.VMEM((2, tokens, half), BF16),
        pltpu.VMEM((2, tokens, half), BF16),
    ]
    return pl.pallas_call(
        functools.partial(kernel, n, nh, chunks),
        out_shape=(
            jax.ShapeDtypeStruct((1, er, half), F32),
            jax.ShapeDtypeStruct((1, er, half), F32),
        ),
        in_specs=[vmem, vmem, vmem, pl.BlockSpec(memory_space=pl.ANY), vmem, vmem, vmem],
        out_specs=(vmem, vmem),
        scratch_shapes=[
            pltpu.VMEM((group * nh, width), F32),
            pltpu.VMEM((n, br, width), F32),
            pltpu.VMEM((n, br, width), F32),
            pltpu.VMEM((tokens, width), F32),
            pltpu.VMEM((tokens, width), BF16),
            pltpu.VMEM((tokens, width), BF16),
            *feat,
            *feat,
            pltpu.VMEM((2, 2, rows, half), F32),
            pltpu.VMEM((2, rows, half), F32),
            pltpu.VMEM((2, rows, half), F32),
            pltpu.VMEM((2, rows, half), F32),
            pltpu.VMEM((2, rows, half), F32),
            pltpu.VMEM((2, 2, rows, half), F32),
            pltpu.VMEM((2, tokens, half), F32),
            pltpu.VMEM((2, width, half), F32),
            pltpu.VMEM((2, n, er, half), F32),
            dma((2, nh)),
            dma((2, n)),
            dma((2, 2, count)),
            dma((2, 2, count)),
            dma((2, 2, count)),
            dma((2, 2, n)),
            dma((1,)),
        ],
        compiler_params=pltpu.CompilerParams(
            collective_id=0, has_side_effects=True, vmem_limit_bytes=56 * 2**20
        ),
    )(query_rows, key_rows, value_rows, teacher_out,
      query_map.reshape(width, half), key_map.reshape(width, half), block_map)


def solution(mesh):
    placed = (
        P("seq", "head"),
        P("seq", "head"),
        P("seq", "head"),
        P(("seq", "head"), None),
        P("head", None, None),
        P("head", None, None),
        P(),
    )
    return jax.shard_map(
        functools.partial(per_device, mesh.shape["seq"], mesh.shape["head"]),
        mesh=mesh,
        in_specs=placed,
        out_specs=(P("head", "seq", None), P("head", "seq", None)),
        check_vma=False,
    )
```

```python
import functools

import jax
import jax.numpy as jnp
from jax import lax
from jax.experimental import pallas as pl
from jax.experimental.pallas import tpu as pltpu
from jax.sharding import PartitionSpec as P

MESH = pl.DeviceIdType.MESH
F32 = jnp.float32
BF16 = jnp.bfloat16
CH = 11
EARLY = 3
NN = (((1,), (0,)), ((), ()))
NT = (((1,), (1,)), ((), ()))
TN = (((0,), (0,)), ((), ()))


def split(x):
    hi = x.astype(BF16)
    return hi, (x - hi.astype(F32)).astype(BF16)


def dot3(a, b, dims):
    one = functools.partial(
        lax.dot_general, dimension_numbers=dims, preferred_element_type=F32
    )
    return one(a[0], b[0]) + (one(a[0], b[1]) + one(a[1], b[0]))


def chunk_bounds(rows, count):
    units = rows // 8
    edges = [8 * (units * i // count) for i in range(count + 1)]
    return [(edges[i], edges[i + 1] - edges[i]) for i in range(count)]


def kernel(
    n, nh, chunks,
    q_ref, k_ref, v_ref, t_ref, qm_ref, km_ref, bm_ref,
    oq_ref, ok_ref,
    gath, t_send, t_arr, teach,
    vh, vl, fk, fkh, fkl, fq, fqh, fql,
    own, x1, part, chain, give, prev,
    grad_k, terms, rs,
    sem_t1, sem_t2, sem_x1, sem_p, sem_x2, sem_rs, sem_loc,
):
    tokens, width = q_ref.shape
    half = fk.shape[2]
    br = tokens // n
    group = t_ref.shape[0]
    er = width // n
    me = lax.axis_index("seq")
    mh = lax.axis_index("head")
    inner = 2
    outer = n // inner
    z = me // inner
    c = me % inner

    def seq_dev(i):
        return (i, mh)

    barrier = pltpu.get_barrier_semaphore()
    for d in range(1, n):
        pl.semaphore_signal(
            barrier, inc=1, device_id=seq_dev((me + d) % n), device_id_type=MESH
        )
    for d in range(1, nh):
        pl.semaphore_signal(
            barrier, inc=1, device_id=(me, (mh + d) % nh), device_id_type=MESH
        )
    pl.semaphore_wait(barrier, n - 1 + nh - 1)

    def t1_copy(to, frm):
        cols = pl.ds(pl.multiple_of(to * width, 128), width)
        return pltpu.make_async_remote_copy(
            src_ref=t_ref.at[:, cols],
            dst_ref=gath.at[pl.ds(pl.multiple_of(frm * group, 8), group), :],
            send_sem=sem_t1.at[0, to],
            recv_sem=sem_t1.at[1, frm],
            device_id=(me, to),
            device_id_type=MESH,
        )

    for d in range(1, nh):
        t1_copy((mh + d) % nh, mh).start()
    t1_own = pltpu.make_async_copy(
        t_ref.at[:, pl.ds(pl.multiple_of(mh * width, 128), width)],
        gath.at[pl.ds(pl.multiple_of(mh * group, 8), group), :],
        sem_loc.at[0],
    )
    t1_own.start()

    def features(rows_ref, map_ref, f, fh, fl):
        pre = jnp.dot(
            rows_ref[...], map_ref[...], precision=lax.Precision.HIGHEST,
            preferred_element_type=F32,
        )
        up = jnp.exp(pre - jnp.max(pre, axis=-1, keepdims=True))
        p1 = up / jnp.sum(up, axis=-1, keepdims=True)
        down = jnp.exp(jnp.min(pre, axis=-1, keepdims=True) - pre)
        p2 = down / jnp.sum(down, axis=-1, keepdims=True)
        for i, p in enumerate((p1, p2)):
            hi, lo = split(p)
            f[i] = p
            fh[i] = hi
            fl[i] = lo

    partner = seq_dev(z * inner + 1 - c)

    def swap_copy(way, i):
        rows = pl.ds(*chunks[i])
        return pltpu.make_async_remote_copy(
            src_ref=own.at[way, 1 - c, rows], dst_ref=x1.at[way, rows],
            send_sem=sem_x1.at[way, 0, i], recv_sem=sem_x1.at[way, 1, i],
            device_id=partner, device_id_type=MESH,
        )

    def onward_copy(way, i):
        rows = pl.ds(*chunks[i])
        zn = lax.rem(z + (1 if way == 0 else outer - 1), outer)
        return pltpu.make_async_remote_copy(
            src_ref=chain.at[way, rows], dst_ref=part.at[way, rows],
            send_sem=sem_p.at[way, 0, i], recv_sem=sem_p.at[way, 1, i],
            device_id=seq_dev(zn * inner + c), device_id_type=MESH,
        )

    def across_copy(way, i, which):
        rows = pl.ds(*chunks[i])
        return pltpu.make_async_remote_copy(
            src_ref=give.at[way, rows], dst_ref=prev.at[way, which, rows],
            send_sem=sem_x2.at[way, 0, i], recv_sem=sem_x2.at[way, 1, i],
            device_id=partner, device_id_type=MESH,
        )

    def scan_begin(way):
        for i in range(len(chunks)):
            swap_copy(way, i).start()

    def scan_run(way):
        place = z if way == 0 else outer - 1 - z
        leads = (c if way == 0 else 1 - c) == 0

        @pl.when(place == 0)
        def _():
            part[way] = jnp.zeros(part.shape[1:], F32)

        for i in range(len(chunks)):
            at, size = chunks[i]
            rows = pl.ds(at, size)
            swap_copy(way, i).wait_recv()

            @pl.when(place > 0)
            def _():
                onward_copy(way, i).wait_recv()

            @pl.when(place < outer - 1)
            def _():
                chain[way, rows] = part[way, rows] + (own[way, c, rows] + x1[way, rows])
                onward_copy(way, i).start()

            before = part[way, rows]
            give[way, rows] = before + jnp.where(leads, own[way, c, rows], 0.0)
            across_copy(way, i, c).start()
            prev[way, c, rows] = before + jnp.where(leads, 0.0, x1[way, rows])

    def scan_end(way):
        place = z if way == 0 else outer - 1 - z
        for i in range(len(chunks)):
            across_copy(way, i, 1 - c).wait_recv()
            swap_copy(way, i).wait_send()
            across_copy(way, i, c).wait_send()

            @pl.when(place < outer - 1)
            def _():
                onward_copy(way, i).wait_send()

    def put_state(way, which, value, norm):
        own[way, which, 0:width] = value
        own[way, which, width:width + 8] = jnp.broadcast_to(norm, (8, half))

    features(k_ref, km_ref, fk, fkh, fkl)
    v_hi, v_lo = split(v_ref[...])
    vh[...] = v_hi
    vl[...] = v_lo

    def key_state(which):
        put_state(
            0, which,
            dot3((vh[...], vl[...]), (fkh[which], fkl[which]), TN),
            jnp.sum(fk[which], axis=0, keepdims=True),
        )

    key_state(1 - c)
    scan_begin(0)
    key_state(c)


    def t2_copy(to, frm):
        return pltpu.make_async_remote_copy(
            src_ref=t_send.at[to],
            dst_ref=t_arr.at[frm],
            send_sem=sem_t2.at[0, to],
            recv_sem=sem_t2.at[1, frm],
            device_id=seq_dev(to),
            device_id_type=MESH,
        )

    def t2_ready():
        for d in range(1, nh):
            frm = (mh + d) % nh
            t1_copy(frm, frm).wait_recv()
        t1_own.wait()

    def t2_fill(d):
        mine = bm_ref[pl.ds(me, 1), :]
        to = (me + d) % n
        held = ((mine >= to * n) & (mine < to * n + n)).astype(F32)
        block = jnp.zeros((br, width), F32)
        for j in range(n):
            block = block + held[:, j:j + 1] * gath[j * br:(j + 1) * br]
        if d == 0:
            t_arr[me] = block
        else:
            t_send[to] = block

    soon = z < EARLY

    @pl.when(soon)
    def _():
        scan_run(0)

    t2_ready()
    for d in range(n):
        t2_fill(d)
        if d > 0:
            to = (me + d) % n

            @pl.when(soon | (to // inner < z))
            def _():
                t2_copy(to, me).start()

    features(q_ref, qm_ref, fq, fqh, fql)
    causal = (
        lax.broadcasted_iota(jnp.int32, (tokens, tokens), 0)
        >= lax.broadcasted_iota(jnp.int32, (tokens, tokens), 1)
    )
    scores = dot3((fqh[0], fql[0]), (fkh[0], fkl[0]), NT)
    scores = scores + dot3((fqh[1], fql[1]), (fkh[1], fkl[1]), NT)
    scores = jnp.where(causal, scores, 0.0)
    numerator = dot3(split(scores), (vh[...], vl[...]), NN)
    raw_sum = jnp.sum(scores, axis=-1, keepdims=True)

    @pl.when(jnp.logical_not(soon))
    def _():
        scan_run(0)
        for d in range(1, n):
            to = (me + d) % n

            @pl.when(to // inner >= z)
            def _():
                t2_copy(to, me).start()

    scan_end(0)

    for i in range(2):
        numerator = numerator + dot3(
            (fqh[i], fql[i]), split(prev[0, i, 0:width]), NT
        )
        raw_sum = raw_sum + jnp.sum(
            fq[i] * prev[0, i, width:width + 1], axis=-1, keepdims=True
        )
    divisor = jnp.maximum(raw_sum, 1.0)
    student = numerator / divisor

    for d in range(1, n):
        frm = (me + d) % n
        t2_copy(frm, frm).wait_recv()
    table = bm_ref[...]
    owned = (table >= me * n) & (table < me * n + n)
    within = jnp.sum(
        jnp.where(owned, table - me * n, 0).astype(F32), axis=1, keepdims=True
    )
    for w in range(n):
        found = (within == w).astype(F32)
        block = jnp.zeros((br, width), F32)
        for s in range(n):
            block = block + found[s:s + 1, :] * t_arr[s]
        teach[w * br:(w + 1) * br] = block

    mismatch = student - teach[...]
    grad_num = mismatch / divisor
    grad_div = jnp.where(
        raw_sum > 1.0,
        -jnp.sum(mismatch * student, axis=-1, keepdims=True) / divisor,
        0.0,
    )
    gn = split(grad_num)

    def query_state(which):
        put_state(
            1, which,
            dot3(gn, (fqh[which], fql[which]), TN),
            jnp.sum(grad_div * fq[which], axis=0, keepdims=True),
        )

    query_state(1 - c)
    scan_begin(1)
    query_state(c)

    soon_back = outer - 1 - z < EARLY

    @pl.when(soon_back)
    def _():
        scan_run(1)

    weights = dot3(gn, (vh[...], vl[...]), NT) + grad_div
    w_parts = split(jnp.where(causal, weights, 0.0))
    grad_q = []
    for i in range(2):
        g = dot3(w_parts, (fkh[i], fkl[i]), NN)
        g = g + dot3(gn, split(prev[0, i, 0:width]), NN)
        grad_q.append(g + grad_div * prev[0, i, width:width + 1])

    def back_pair(f, g1, g2):
        p1, p2 = f[0], f[1]
        lead = p1 * (g1 - jnp.sum(p1 * g1, axis=-1, keepdims=True))
        trail = p2 * (g2 - jnp.sum(p2 * g2, axis=-1, keepdims=True))
        return lead - trail

    def rs_copy(i, to, frm):
        return pltpu.make_async_remote_copy(
            src_ref=terms.at[i, pl.ds(pl.multiple_of(to * er, 8), er), :],
            dst_ref=rs.at[i, frm],
            send_sem=sem_rs.at[i, 0, to],
            recv_sem=sem_rs.at[i, 1, frm],
            device_id=seq_dev(to),
            device_id_type=MESH,
        )

    def rs_term(i, rows_ref, grad):
        terms[i] = dot3(split(rows_ref[...]), split(grad), TN)

    def rs_finish(i, out_ref):
        total = terms[i, pl.ds(pl.multiple_of(me * er, 8), er), :]
        for d in range(1, n):
            frm = (me + d) % n
            rs_copy(i, frm, frm).wait_recv()
            total = total + rs[i, frm]
        out_ref[0] = total

    rs_term(0, q_ref, back_pair(fq, grad_q[0], grad_q[1]))
    for d in range(1, n):
        to = (me + d) % n

        @pl.when(soon_back | (to // inner > z))
        def _():
            rs_copy(0, to, me).start()

    for i in range(2):
        grad_k[i] = dot3(w_parts, (fqh[i], fql[i]), TN)

    @pl.when(jnp.logical_not(soon_back))
    def _():
        scan_run(1)
        for d in range(1, n):
            to = (me + d) % n

            @pl.when(to // inner <= z)
            def _():
                rs_copy(0, to, me).start()

    scan_end(1)

    grads = []
    for i in range(2):
        g = grad_k[i] + dot3((vh[...], vl[...]), split(prev[1, i, 0:width]), NN)
        grads.append(g + prev[1, i, width:width + 1])
    rs_term(1, k_ref, back_pair(fk, grads[0], grads[1]))
    for d in range(1, n):
        rs_copy(1, (me + d) % n, me).start()
    rs_finish(0, oq_ref)
    rs_finish(1, ok_ref)

    for d in range(1, nh):
        t1_copy((mh + d) % nh, mh).wait_send()
    for d in range(1, n):
        to = (me + d) % n
        t2_copy(to, me).wait_send()
        rs_copy(0, to, me).wait_send()
        rs_copy(1, to, me).wait_send()


def per_device(n, nh, query_rows, key_rows, value_rows, teacher_out, query_map, key_map, block_map):
    tokens, width = query_rows.shape
    half = query_map.shape[2]
    group = teacher_out.shape[0]
    er = width // n
    br = tokens // n
    rows = width + 8
    chunks = chunk_bounds(rows, CH)
    count = len(chunks)
    vmem = pl.BlockSpec(memory_space=pltpu.VMEM)
    dma = pltpu.SemaphoreType.DMA
    feat = [
        pltpu.VMEM((2, tokens, half), F32),
        pltpu.VMEM((2, tokens, half), BF16),
        pltpu.VMEM((2, tokens, half), BF16),
    ]
    return pl.pallas_call(
        functools.partial(kernel, n, nh, chunks),
        out_shape=(
            jax.ShapeDtypeStruct((1, er, half), F32),
            jax.ShapeDtypeStruct((1, er, half), F32),
        ),
        in_specs=[vmem, vmem, vmem, pl.BlockSpec(memory_space=pl.ANY), vmem, vmem, vmem],
        out_specs=(vmem, vmem),
        scratch_shapes=[
            pltpu.VMEM((group * nh, width), F32),
            pltpu.VMEM((n, br, width), F32),
            pltpu.VMEM((n, br, width), F32),
            pltpu.VMEM((tokens, width), F32),
            pltpu.VMEM((tokens, width), BF16),
            pltpu.VMEM((tokens, width), BF16),
            *feat,
            *feat,
            pltpu.VMEM((2, 2, rows, half), F32),
            pltpu.VMEM((2, rows, half), F32),
            pltpu.VMEM((2, rows, half), F32),
            pltpu.VMEM((2, rows, half), F32),
            pltpu.VMEM((2, rows, half), F32),
            pltpu.VMEM((2, 2, rows, half), F32),
            pltpu.VMEM((2, tokens, half), F32),
            pltpu.VMEM((2, width, half), F32),
            pltpu.VMEM((2, n, er, half), F32),
            dma((2, nh)),
            dma((2, n)),
            dma((2, 2, count)),
            dma((2, 2, count)),
            dma((2, 2, count)),
            dma((2, 2, n)),
            dma((1,)),
        ],
        compiler_params=pltpu.CompilerParams(
            collective_id=0, has_side_effects=True, vmem_limit_bytes=56 * 2**20
        ),
    )(query_rows, key_rows, value_rows, teacher_out,
      query_map.reshape(width, half), key_map.reshape(width, half), block_map)


def solution(mesh):
    placed = (
        P("seq", "head"),
        P("seq", "head"),
        P("seq", "head"),
        P(("seq", "head"), None),
        P("head", None, None),
        P("head", None, None),
        P(),
    )
    return jax.shard_map(
        functools.partial(per_device, mesh.shape["seq"], mesh.shape["head"]),
        mesh=mesh,
        in_specs=placed,
        out_specs=(P("head", "seq", None), P("head", "seq", None)),
        check_vma=False,
    )
```
